32 devices in a mesh: dp: 16 (over z, x, core), expert: 2 (over y).
Axes of the slice: x: 2, y: 2, z: 4, core: 2. Of those that a mesh axis runs over, the one named last changes fastest.
Arguments:
- acts: bfloat16 [8192, 8, 1024], P(('dp', 'expert')), may hold values from -6 to 6
- grads: bfloat16 [8192, 2048], P(('dp', 'expert')), may hold values from -6 to 6
- probs: float32 [8192, 8], P(('dp', 'expert')), may hold values from 0.02 to 0.3
- expert_ids: int32 [8192, 8], P(('dp', 'expert')), may hold values from 0 to 63, as said below
- example_ids: int32 [16, 512], P('dp', 'expert'), may hold values from 0 to 2, never falling along the last dimension, each value on 1 to 256 neighbouring positions
- act_basis: bfloat16 [2, 1024, 1024], P('expert', 'dp'), may hold values from -0.1875 to 0.1875
- grad_basis: bfloat16 [2, 2048, 2048], P('expert', 'dp'), may hold values from -0.125 to 0.125
Outputs:
- eigenvalues: float32 [2, 1024, 2048], P('expert', 'dp')
The draws below stay inside these ranges and needn't reach their ends.
Inputs may be any that keep to these rules, and one draw needn't show every extreme that they name: `expert_ids`: each token names 8 different experts. Experts 0 to 1 form the window. Among the 256 tokens of one device every window expert is named by at least one and at most 64 tokens, and one window expert, the same for all devices, is named by exactly 64 tokens of every device.
All inputs are finite; a program needn't handle non-finite values.
Results may differ from the reference program's by a relative error of at most 0.004.
Values may be sent and summed in bfloat16 or wider, within the bound.
A program may use at most 64 MiB of HBM per device.

```python
import math
from functools import partial
import jax
import jax.numpy as jnp
import numpy as np
from jax import lax

D = 2048
FF = 1024
EXPERTS = 64
TOPK = 8
TOK_DEV = 256
EXAMPLES = 3
CAP = 64
WIN = 2
GROUP_TOK = 512
TOKENS = 8192
ROWS = 128
EX_MOST = 256
N_DP = 16
N_EXPERT = 2


def draw_expert_ids(key, part):
    blocks = TOKENS // TOK_DEV
    spare = EXPERTS - WIN
    key_top, key_level, key_jitter, key_rank, key_rest = jax.random.split(key, 5)
    heavy = jax.random.randint(key_top, (), 0, WIN)
    window = jnp.arange(WIN, dtype=jnp.int32)
    level = 1 + jax.random.randint(key_level, (WIN,), 0, 2)
    jitter = jax.random.randint(key_jitter, (blocks, WIN), 0, CAP // 16 + 1)
    counts = jnp.where(window[None, :] == heavy, CAP, CAP * level[None, :] // 4 - jitter)
    scores = jax.random.randint(key_rank, (blocks, WIN, TOK_DEV), 0, 1 << 16) * TOK_DEV + jnp.arange(TOK_DEV, dtype=jnp.int32)
    order = jnp.argsort(scores, axis=-1)
    ranked = jnp.argsort(order, axis=-1)
    member = (ranked < counts[:, :, None]).astype(jnp.int32)
    member = jnp.transpose(member, (0, 2, 1))
    named = jnp.sum(member, axis=-1, dtype=jnp.int32)
    order_score = member * (2 * WIN) + (WIN - 1 - window)[None, None, :]
    _, first_ids = lax.top_k(order_score, WIN)
    if WIN < TOPK:
        first_ids = jnp.concatenate([first_ids, jnp.zeros((blocks, TOK_DEV, TOPK - WIN), jnp.int32)], axis=-1)
    rest_scores = jax.random.randint(key_rest, (blocks, TOK_DEV, spare), 0, 1 << 16) * spare + jnp.arange(spare, dtype=jnp.int32)
    _, rest_ids = lax.top_k(rest_scores, TOPK)
    slots = jnp.arange(TOPK, dtype=jnp.int32)
    from_rest = jnp.take_along_axis(rest_ids, jnp.clip(slots[None, None, :] - named[:, :, None], 0, TOPK - 1), axis=-1) + WIN
    chosen = jnp.where(slots[None, None, :] < named[:, :, None], first_ids, from_rest)
    return chosen.reshape(blocks * TOK_DEV, TOPK).astype(jnp.int32)


def block_levels(key, extent, cuts, smallest, high):
    factor_of, own = 1.0, jax.random.fold_in(key, 6)
    for position, shards_of in cuts:
        steps = jnp.exp(jax.random.uniform(jax.random.fold_in(own, position), (shards_of,), jnp.float32, smallest / len(cuts), high / len(cuts)))
        factor_of = factor_of * jnp.repeat(steps, extent[position] // shards_of).reshape([-1 if axis == position else 1 for axis in range(len(extent))])
    return factor_of


def profile(amount, total, limit, slope):
    weights = [(1 << 20) // math.isqrt(rank ** slope) + 1 for rank in range(2, amount + 1)]
    spare, given = total - limit - (amount - 1), [1] * (amount - 1)
    while spare > 0:
        candidates = [i for i in range(amount - 1) if given[i] < limit]
        pool, remaining = sum([weights[i] for i in candidates]), spare
        for i in candidates:
            addition = min(limit - given[i], max(1, remaining * weights[i] // pool), spare)
            given[i] = given[i] + addition
            spare = spare - addition
    return np.array([limit] + given)


def uneven(stream_key, count, total, limit, skew):
    if count == 2:
        one = jax.random.randint(stream_key, (), max(1, total - limit), min(limit, total - 1) + 1)
        return jnp.stack([one, total - one])
    sizes = jnp.asarray(profile(count, total, limit, skew), jnp.int32)
    pairs = (count - 1) // 2
    giver, receiver = sizes[1:1 + 2 * pairs:2], sizes[2:2 + 2 * pairs:2]
    slack = jnp.minimum(giver - 1, limit - receiver)
    shifted = jax.random.randint(jax.random.fold_in(stream_key, 1), (pairs,), 0, 1 << 20) % (slack + 1)
    sizes = sizes.at[1:1 + 2 * pairs:2].set(giver - shifted).at[2:2 + 2 * pairs:2].set(receiver + shifted)
    return sizes[jax.random.permutation(jax.random.fold_in(stream_key, 2), count)]


def noise(stream_key, extent, scale, reach, shards=(), kind=jnp.bfloat16):
    values = jax.random.normal(stream_key, extent, jnp.float32) * scale
    if len(shards) > 0:
        values = block_levels(stream_key, extent, shards, -0.22, 0.18) * values
    return jnp.clip(values, min=-reach, max=reach).astype(kind)


def setup_inputs(seed: int = 0) -> dict:
    key_of = jax.random.split(jax.random.key(seed), 8)
    return {
        "acts": noise(key_of[0], (TOKENS, TOPK, FF), 1.0, 6.0, ((0, 32),)),
        "grads": noise(key_of[1], (TOKENS, D), 1.0, 6.0, ((0, 32),)),
        "probs": jnp.clip(jnp.exp(math.log(0.3) - 2.7080503 * jax.random.uniform(key_of[2], (TOKENS, TOPK), jnp.float32) ** block_levels(key_of[2], (TOKENS, TOPK), ((0, 32),), -0.2, 0.2)), 0.02, 0.3),
        "expert_ids": draw_expert_ids(jax.random.fold_in(key_of[7], 71), 0),
        "example_ids": jax.vmap(lambda own: jnp.searchsorted(jnp.cumsum(uneven(own, EXAMPLES, GROUP_TOK, EX_MOST, 1)), jnp.arange(GROUP_TOK), side="right"))(jax.random.split(key_of[4], N_DP)).reshape((N_DP, GROUP_TOK)).astype(jnp.int32),
        "act_basis": noise(key_of[5], (WIN, FF, FF), FF ** -0.5, 0.1875, ((0, 2), (1, 16))),
        "grad_basis": noise(key_of[6], (WIN, D, D), D ** -0.5, 0.125, ((0, 2), (1, 16))),
    }


def route_block(picked, activity, weights, gradient, labels, expert):
    count_tok = picked.shape[0]
    count_slot = picked.shape[1]
    capacity = count_tok // 4
    names = (picked == expert).astype(jnp.int32)
    named = jnp.sum(names, axis=1, dtype=jnp.int32)
    which = jnp.sum(names * jnp.arange(count_slot, dtype=jnp.int32)[None, :], axis=1, dtype=jnp.int32)
    ranked = jnp.cumsum(named, dtype=jnp.int32) - 1
    places = jnp.arange(capacity, dtype=jnp.int32)
    table = ((ranked[None, :] == places[:, None]) & (named[None, :] == 1)).astype(jnp.int32)
    token = jnp.sum(table * jnp.arange(count_tok, dtype=jnp.int32)[None, :], axis=1, dtype=jnp.int32)
    filled = jnp.sum(table, axis=1, dtype=jnp.int32)
    flat_index = token * count_slot + which[token]
    rows_acts = activity.reshape(count_tok * count_slot, activity.shape[-1])[flat_index] * filled[:, None].astype(activity.dtype)
    scaled = weights.reshape(count_tok * count_slot)[flat_index] * filled.astype(weights.dtype)
    rows_grads = (scaled[:, None] * gradient[token].astype(jnp.float32)).astype(jnp.bfloat16)
    example_range = jnp.arange(EXAMPLES, dtype=jnp.int32)
    member = ((labels[token][:, None] == example_range[None, :]) & (filled[:, None] == 1)).astype(jnp.bfloat16)
    return rows_acts, rows_grads, member


def reference(acts, grads, probs, expert_ids, example_ids, act_basis, grad_basis):
    groups = jnp.arange(N_DP, dtype=jnp.int32)
    results = []
    for expert in range(WIN):
        basis_acts = act_basis[expert]
        basis_grads = grad_basis[expert]

        def add_group(total, group):
            first = group * GROUP_TOK
            picked = lax.dynamic_slice_in_dim(expert_ids, first, GROUP_TOK, 0).reshape(N_EXPERT, TOK_DEV, TOPK)
            activity = lax.dynamic_slice_in_dim(acts, first, GROUP_TOK, 0).reshape(N_EXPERT, TOK_DEV, TOPK, FF)
            weights = lax.dynamic_slice_in_dim(probs, first, GROUP_TOK, 0).reshape(N_EXPERT, TOK_DEV, TOPK)
            gradient = lax.dynamic_slice_in_dim(grads, first, GROUP_TOK, 0).reshape(N_EXPERT, TOK_DEV, D)
            labels = lax.dynamic_index_in_dim(example_ids, group, 0, keepdims=False).reshape(N_EXPERT, TOK_DEV)
            rows_acts, rows_grads, member = jax.vmap(partial(route_block, expert=expert))(picked, activity, weights, gradient, labels)
            rows_acts = rows_acts.reshape(ROWS, FF)
            rows_grads = rows_grads.reshape(ROWS, D)
            member = member.reshape(ROWS, EXAMPLES)
            rotated_acts = jnp.dot(rows_acts, basis_acts, preferred_element_type=jnp.float32).astype(jnp.bfloat16)
            rotated_grads = jnp.dot(rows_grads, basis_grads, preferred_element_type=jnp.float32).astype(jnp.bfloat16)
            masked = member.astype(jnp.float32).T[:, :, None] * rotated_acts.astype(jnp.float32)[None, :, :]
            product = jnp.einsum('jrf,rd->jfd', masked, rotated_grads.astype(jnp.float32), precision=lax.Precision.HIGHEST)
            return total + jnp.sum(product * product, axis=0), None

        total, _ = lax.scan(add_group, jnp.zeros((FF, D), jnp.float32), groups)
        results.append(total)
    return jnp.stack(results) * (1.0 / (EXAMPLES * N_DP))
```

```python
import math

import jax
import jax.numpy as jnp
from jax import lax
from jax.experimental import pallas as pl
from jax.experimental.pallas import tpu as pltpu
from jax.sharding import PartitionSpec as P

EXAMPLES = 3


def route_block(picked, activity, weights, gradient, labels, expert):
    count_tok = picked.shape[0]
    count_slot = picked.shape[1]
    capacity = count_tok // 4
    names = (picked == expert).astype(jnp.int32)
    named = jnp.sum(names, axis=1, dtype=jnp.int32)
    which = jnp.sum(
        names * jnp.arange(count_slot, dtype=jnp.int32)[None, :], axis=1, dtype=jnp.int32
    )
    ranked = jnp.cumsum(named, dtype=jnp.int32) - 1
    places = jnp.arange(capacity, dtype=jnp.int32)
    table = ((ranked[None, :] == places[:, None]) & (named[None, :] == 1)).astype(jnp.int32)
    token = jnp.sum(
        table * jnp.arange(count_tok, dtype=jnp.int32)[None, :], axis=1, dtype=jnp.int32
    )
    filled = jnp.sum(table, axis=1, dtype=jnp.int32)
    flat_index = token * count_slot + which[token]
    rows_acts = activity.reshape(count_tok * count_slot, activity.shape[-1])[flat_index] * filled[
        :, None
    ].astype(activity.dtype)
    scaled = weights.reshape(count_tok * count_slot)[flat_index] * filled.astype(weights.dtype)
    rows_grads = (scaled[:, None] * gradient[token].astype(jnp.float32)).astype(jnp.bfloat16)
    example_range = jnp.arange(EXAMPLES, dtype=jnp.int32)
    member = ((labels[token][:, None] == example_range[None, :]) & (filled[:, None] == 1)).astype(
        jnp.bfloat16
    )
    return (rows_acts, rows_grads, member)


def body(acts, grads, probs, expert_ids, example_ids, act_basis, grad_basis):
    owners = lax.axis_size("expert")
    shards = lax.axis_size("dp")
    hidden_width = acts.shape[2]
    model_width = grads.shape[1]
    labels = example_ids[0]
    experts = jnp.arange(owners, dtype=jnp.int32)

    def route_one(expert):
        return route_block(expert_ids, acts, probs, grads, labels, expert)

    send_acts, send_grads, send_member = jax.vmap(route_one)(experts)
    got_acts, got_grads, got_member = (
        lax.all_to_all(send_acts, "expert", split_axis=0, concat_axis=0, tiled=True),
        lax.all_to_all(send_grads, "expert", split_axis=0, concat_axis=0, tiled=True),
        lax.all_to_all(send_member, "expert", split_axis=0, concat_axis=0, tiled=True),
    )
    routed_acts = got_acts.reshape(-1, hidden_width)
    routed_grads = got_grads.reshape(-1, model_width)
    member = got_member.reshape(-1, got_member.shape[-1])
    basis_acts = act_basis[0]
    basis_grads = grad_basis[0]
    full_acts, full_grads = (
        lax.all_gather(basis_acts, "dp", axis=0, tiled=True),
        lax.all_gather(basis_grads, "dp", axis=0, tiled=True),
    )
    rotated_acts = jnp.dot(routed_acts, full_acts, preferred_element_type=jnp.float32).astype(
        jnp.bfloat16
    )
    rotated_grads = jnp.dot(routed_grads, full_grads, preferred_element_type=jnp.float32).astype(
        jnp.bfloat16
    )
    scale = 1.0 / (member.shape[-1] * shards)
    member_first = member.T
    width_step = math.gcd(hidden_width, 256)
    pieces = []
    for offset in range(0, hidden_width, width_step):
        columns = lax.dynamic_slice_in_dim(rotated_acts, 0 + offset, width_step, 1)
        masked = member_first[:, :, None] * columns[None, :, :]
        product = jnp.einsum(
            "jrf,rd->jfd", masked, rotated_grads, preferred_element_type=jnp.float32
        )
        pieces.append(jnp.sum(product * product, axis=0))
    totals = jnp.concatenate(pieces, axis=0) * scale
    result = lax.psum_scatter(totals, "dp", scatter_dimension=0, tiled=True)
    return result[None]


NZ = 4
CHUNK = 512


def kernel(
    ids_ref, probs_ref, labels_ref, acts_ref, grads_ref, act_basis_ref, grad_basis_ref, out_ref,
    full_acts, full_grads, send_a, send_g, send_m, rows_a, rows_g, rows_m, masked,
    acc, core_out, core_in, x_out, x_in, up_out, up_in, down_out, down_in,
    y_send, y_recv, g_send, g_recv, r_send, r_recv,
):
    me = lax.axis_index("dp")
    own = lax.axis_index("expert")
    core = lax.rem(me, 2)
    x = lax.rem(me // 2, 2)
    z = me // 4
    chunks = full_grads.shape[0]
    tall = grad_basis_ref.shape[0]
    short = act_basis_ref.shape[0]
    block = out_ref.shape[0]
    capacity = send_a.shape[0]
    bf16, f32 = jnp.bfloat16, jnp.float32

    def at(zz, xx, cc):
        return {"dp": (zz * 2 + xx) * 2 + cc}

    sibling, beside = at(z, x, 1 - core), at(z, 1 - x, core)
    above, below = at(z + 1, x, core), at(z - 1, x, core)
    partner = {"expert": 1 - own}

    barrier = pltpu.get_barrier_semaphore()
    for target in (sibling, beside, partner):
        pl.semaphore_signal(barrier, inc=1, device_id=target, device_id_type=pl.DeviceIdType.MESH)

    @pl.when(z < NZ - 1)
    def _():
        pl.semaphore_signal(barrier, inc=1, device_id=above, device_id_type=pl.DeviceIdType.MESH)

    @pl.when(z > 0)
    def _():
        pl.semaphore_signal(barrier, inc=1, device_id=below, device_id_type=pl.DeviceIdType.MESH)

    ends = (z == 0).astype(jnp.int32) + (z == NZ - 1).astype(jnp.int32)
    pl.semaphore_wait(barrier, 5 - ends)

    def remote(src, dst, ssem, rsem, target):
        return pltpu.make_async_remote_copy(
            src_ref=src, dst_ref=dst, send_sem=ssem, recv_sem=rsem,
            device_id=target, device_id_type=pl.DeviceIdType.MESH,
        )

    def shard(part, zz, xx, cc):
        index = (zz * 2 + xx) * 2 + cc
        if part == 0:
            return full_acts.at[pl.ds(pl.multiple_of(index * short, short), short), :]
        return full_grads.at[part - 1, pl.ds(pl.multiple_of(index * tall, tall), tall), :]

    full_acts[pl.ds(pl.multiple_of(me * short, short), short), :] = act_basis_ref[...]
    for k in range(chunks):
        full_grads[k, pl.ds(pl.multiple_of(me * tall, tall), tall), :] = grad_basis_ref[
            :, k * CHUNK : (k + 1) * CHUNK
        ]

    def item_z(item):
        if item == 0:
            return z
        return z - item if item < NZ else z + (item - NZ + 1)

    def present(item):
        if item == 0:
            return z >= 0
        return z >= item if item < NZ else z + (item - NZ + 1) <= NZ - 1

    def copy_up(part, item):
        ref = shard(part, item_z(item), x, core)
        return remote(ref, ref, g_send.at[part, item], g_recv.at[part, item + 1], above)

    def copy_down(part, item):
        new = NZ if item == 0 else item + 1
        ref = shard(part, item_z(item), x, core)
        return remote(ref, ref, g_send.at[part, 3 + new], g_recv.at[part, new], below)

    def copy_beside(part, item):
        ref = shard(part, item_z(item), x, core)
        return remote(ref, ref, g_send.at[part, 10 + item], g_recv.at[part, 7 + item], beside)

    def copy_sibling(part, item):
        ref = shard(part, item_z(item), x, core)
        return remote(ref, ref, g_send.at[part, 17 + item], g_recv.at[part, 14 + item], sibling)

    def copy_sibling_far(part, item):
        ref = shard(part, item_z(item), 1 - x, core)
        return remote(ref, ref, g_send.at[part, 24 + item], g_recv.at[part, 21 + item], sibling)

    def came(part, item, slot, zz, xx, cc):
        ref = shard(part, zz, xx, cc)
        remote(ref, ref, g_send.at[part, 0], g_recv.at[part, slot], sibling).wait_recv()

    def goes_up(item):
        return jnp.logical_and(present(item), z < NZ - 1)

    def goes_down(item):
        return jnp.logical_and(present(item), z > 0)

    def pass_on(part, item):
        @pl.when(present(item))
        def _():
            if item > 0:
                came(part, item, item, item_z(item), x, core)
            copy_beside(part, item).start()

        if item < NZ - 1:
            @pl.when(goes_up(item))
            def _():
                copy_up(part, item).start()

        if item == 0 or NZ <= item < 2 * NZ - 2:
            @pl.when(goes_down(item))
            def _():
                copy_down(part, item).start()

        @pl.when(present(item))
        def _():
            copy_sibling(part, item).start()

    def pass_far(part, item):
        @pl.when(present(item))
        def _():
            came(part, item, 7 + item, item_z(item), 1 - x, core)
            copy_sibling_far(part, item).start()

    def hop(part, h):
        for item in ((0,) if h == 0 else (h, NZ - 1 + h)):
            pass_on(part, item)

    def hop_far(part, h):
        for item in ((0,) if h == 0 else (h, NZ - 1 + h)):
            pass_far(part, item)

    def gathered(part):
        for item in range(2 * NZ - 1):
            @pl.when(present(item))
            def _():
                came(part, item, 14 + item, item_z(item), x, 1 - core)
                came(part, item, 21 + item, item_z(item), 1 - x, 1 - core)

    def drain(part):
        for item in range(2 * NZ - 1):
            @pl.when(present(item))
            def _():
                copy_beside(part, item).wait_send()
                copy_sibling(part, item).wait_send()
                copy_sibling_far(part, item).wait_send()

            if item < NZ - 1:
                @pl.when(goes_up(item))
                def _():
                    copy_up(part, item).wait_send()

            if item == 0 or NZ <= item < 2 * NZ - 2:
                @pl.when(goes_down(item))
                def _():
                    copy_down(part, item).wait_send()

    def route():
        lane = lax.broadcasted_iota(jnp.int32, (128, 128), 1)
        row = lax.broadcasted_iota(jnp.int32, (128, 128), 0)
        earlier = (row < lane).astype(bf16)
        lines = ids_ref.shape[0]
        above_line = (
            lax.broadcasted_iota(jnp.int32, (lines, lines), 1)
            < lax.broadcasted_iota(jnp.int32, (lines, lines), 0)
        ).astype(bf16)
        slots = slots_of(acts_ref, grads_ref)
        place = lax.broadcasted_iota(jnp.int32, (capacity, 128), 0).astype(f32)
        spot = lax.broadcasted_iota(jnp.int32, (capacity, 128), 1) // slots
        picks, tokens, scales, members = [], [], [], []
        for expert in (1 - own, own):
            hit = jnp.where(ids_ref[...] == expert, 1.0, 0.0)
            inside = jnp.dot(hit.astype(bf16), earlier, preferred_element_type=f32)
            each = jnp.broadcast_to(jnp.sum(hit, axis=1, keepdims=True), hit.shape)
            before = jnp.dot(above_line, each.astype(bf16), preferred_element_type=f32)
            key = jnp.where(hit > 0.5, inside + before, -1.0)
            pieces = []
            scale = jnp.zeros((capacity, 128), f32)
            token = jnp.zeros((capacity, 128), jnp.int32)
            for i in range(lines):
                chosen = place == key[i : i + 1, :]
                pieces.append(jnp.where(chosen, 1.0, 0.0).astype(bf16))
                scale = scale + jnp.where(chosen, probs_ref[i : i + 1, :], 0.0)
                token = token + jnp.where(chosen, spot + (i * (128 // slots) + 1), 0)
            scales.append(jnp.sum(scale, axis=1, keepdims=True))
            token = jnp.sum(token, axis=1, keepdims=True) - 1
            wide = lax.broadcasted_iota(jnp.int32, (capacity, grads_ref.shape[0]), 1) == token
            label = jnp.sum(jnp.where(wide, labels_ref[...] + 1, 0), axis=1, keepdims=True) - 1
            member = lax.broadcasted_iota(jnp.int32, (capacity, 128), 1) == label
            members.append(jnp.where(member, 1.0, 0.0).astype(bf16))
            picks.append(jnp.concatenate(pieces, axis=1))
            tokens.append(jnp.where(wide, 1.0, 0.0).astype(bf16))
        a = jnp.dot(jnp.concatenate(picks, axis=0), acts_ref[...], preferred_element_type=f32)
        g = jnp.dot(jnp.concatenate(tokens, axis=0), grads_ref[...], preferred_element_type=f32)
        g = g * jnp.concatenate(scales, axis=0)
        send_a[...] = a[:capacity].astype(bf16)
        send_g[...] = g[:capacity].astype(bf16)
        send_m[...] = members[0]
        for copy in exchange():
            copy.start()
        rows_a[0] = a[capacity:].astype(bf16)
        rows_g[0] = g[capacity:].astype(bf16)
        rows_m[0] = members[1]

    def exchange():
        pairs = ((send_a, rows_a), (send_g, rows_g), (send_m, rows_m))
        return [
            remote(src, dst.at[1], y_send.at[n], y_recv.at[n], partner)
            for n, (src, dst) in enumerate(pairs)
        ]

    def rotate_acts():
        for copy in exchange():
            copy.wait_recv()
        rows = rows_a[...].reshape(2 * capacity, rows_a.shape[2])
        rotated = jnp.dot(rows, full_acts[...], preferred_element_type=f32)
        turned = rotated.T.astype(bf16)
        mask = rows_m[...].reshape(2 * capacity, 128).astype(f32).T.astype(bf16)
        for index in range(4 * NZ):
            zz, xx, cc = index // 4, index // 2 % 2, index % 2
            b = (cc * 2 + xx) * NZ + zz
            part = turned[index * block : (index + 1) * block, :]
            for j in range(EXAMPLES):
                masked[b, j * block : (j + 1) * block, :] = part * mask[j : j + 1, :]

    def core_copy(k):
        return remote(core_out.at[k], core_in.at[k], r_send.at[k, 0], r_recv.at[k, 0], sibling)

    def x_copy(k):
        return remote(x_out.at[k], x_in.at[k], r_send.at[k, 1], r_recv.at[k, 1], beside)

    def up_copy(k, b):
        return remote(
            up_out.at[k, b], up_in.at[k, b], r_send.at[k, 2 + b], r_recv.at[k, 2 + b], above
        )

    def down_copy(k, b):
        return remote(
            down_out.at[k, b], down_in.at[k, b], r_send.at[k, 6 + b], r_recv.at[k, 6 + b], below
        )

    def squares(k):
        rows = rows_g[...].reshape(2 * capacity, rows_g.shape[2])
        rotated = jnp.dot(rows, full_grads[k], preferred_element_type=f32).astype(bf16)

        def total(b):
            product = jnp.dot(masked[b], rotated, preferred_element_type=f32)
            product = product * product
            return product[:block] + product[block : 2 * block] + product[2 * block :]

        @pl.loop(0, 2 * NZ)
        def _(n):
            core_out[k, n] = total((1 - core) * (2 * NZ) + n).astype(bf16)

        core_copy(k).start()

        @pl.loop(0, 2 * NZ)
        def _(n):
            acc[k, n] = total(core * (2 * NZ) + n)

    def to_beside(k):
        core_copy(k).wait_recv()
        far, near = (1 - x) * NZ, x * NZ

        @pl.loop(0, NZ)
        def _(n):
            x_out[k, n] = (acc[k, far + n] + core_in[k, far + n].astype(f32)).astype(bf16)

        x_copy(k).start()

        @pl.loop(0, NZ)
        def _(n):
            acc[k, near + n] = acc[k, near + n] + core_in[k, near + n].astype(f32)

    def to_line(k):
        x_copy(k).wait_recv()
        near = x * NZ

        @pl.loop(0, NZ)
        def _(n):
            acc[k, near + n] = acc[k, near + n] + x_in[k, n].astype(f32)

        for b in range(NZ):
            @pl.when(jnp.logical_and(z == 0, b > z))
            def _():
                up_out[k, b] = acc[k, near + b].astype(bf16)
                up_copy(k, b).start()

            @pl.when(jnp.logical_and(z == NZ - 1, b < z))
            def _():
                down_out[k, b] = acc[k, near + b].astype(bf16)
                down_copy(k, b).start()

    def along(k):
        near = x * NZ

        def up(b):
            @pl.when(jnp.logical_and(z > 0, b > z))
            def _():
                up_copy(k, b).wait_recv()
                up_out[k, b] = (acc[k, near + b] + up_in[k, b].astype(f32)).astype(bf16)
                up_copy(k, b).start()

        def down(b):
            @pl.when(jnp.logical_and(z < NZ - 1, b < z))
            def _():
                down_copy(k, b).wait_recv()
                down_out[k, b] = (acc[k, near + b] + down_in[k, b].astype(f32)).astype(bf16)
                down_copy(k, b).start()

        for b in range(NZ):
            up(NZ - 1 - b)
            down(b)

    def finish(k):
        near = x * NZ
        columns = slice(k * CHUNK, (k + 1) * CHUNK)
        out_ref[:, columns] = acc[k, near + z]
        for b in range(NZ):
            @pl.when(jnp.logical_and(z > 0, z == b))
            def _():
                up_copy(k, b).wait_recv()
                out_ref[:, columns] = out_ref[:, columns] + up_in[k, b].astype(f32)

            @pl.when(jnp.logical_and(z < NZ - 1, z == b))
            def _():
                down_copy(k, b).wait_recv()
                out_ref[:, columns] = out_ref[:, columns] + down_in[k, b].astype(f32)

        out_ref[:, columns] = out_ref[:, columns] * (1.0 / (EXAMPLES * 4 * NZ))

    def drain_sums(k):
        core_copy(k).wait_send()
        x_copy(k).wait_send()
        for b in range(NZ):
            @pl.when(jnp.logical_and(z < NZ - 1, b > z))
            def _():
                up_copy(k, b).wait_send()

            @pl.when(jnp.logical_and(z > 0, b < z))
            def _():
                down_copy(k, b).wait_send()

    parts = chunks + 1
    AHEAD = 1
    for part in range(AHEAD):
        hop(part, 0)
    for step in range(parts + 9):
        if step + AHEAD < parts:
            hop(step + AHEAD, 0)
        if step == 0:
            route()
        for h in range(1, NZ):
            if 0 <= step - h < parts:
                hop(step - h, h)
        for h in range(NZ):
            if 0 <= step - h - 1 < parts:
                hop_far(step - h - 1, h)
        if 0 <= step - NZ < parts:
            gathered(step - NZ)
            if step == NZ:
                rotate_acts()
            else:
                squares(step - NZ - 1)
        if 0 <= step - NZ - 2 < chunks:
            to_beside(step - NZ - 2)
        if 0 <= step - NZ - 3 < chunks:
            to_line(step - NZ - 3)
        if 0 <= step - NZ - 4 < chunks:
            along(step - NZ - 4)
        if 0 <= step - NZ - 5 < chunks:
            finish(step - NZ - 5)
    for copy in exchange():
        copy.wait_send()
    for part in range(parts):
        drain(part)
    for k in range(chunks):
        drain_sums(k)


def slots_of(acts_ref, grads_ref):
    return acts_ref.shape[0] // grads_ref.shape[0]


def fused(acts, grads, probs, expert_ids, example_ids, act_basis, grad_basis):
    tokens, slots, hidden = acts.shape
    model = grads.shape[1]
    capacity = tokens // 4
    chunks = model // CHUNK
    block = hidden // (4 * NZ)
    bf16, f32 = jnp.bfloat16, jnp.float32
    vm = pl.BlockSpec(memory_space=pltpu.VMEM)
    dma = pltpu.SemaphoreType.DMA
    result = pl.pallas_call(
        kernel,
        out_shape=jax.ShapeDtypeStruct((block, model), f32),
        in_specs=[vm] * 7,
        out_specs=vm,
        scratch_shapes=[
            pltpu.VMEM((hidden, hidden), bf16),
            pltpu.VMEM((chunks, model, CHUNK), bf16),
            pltpu.VMEM((capacity, hidden), bf16),
            pltpu.VMEM((capacity, model), bf16),
            pltpu.VMEM((capacity, 128), bf16),
            pltpu.VMEM((2, capacity, hidden), bf16),
            pltpu.VMEM((2, capacity, model), bf16),
            pltpu.VMEM((2, capacity, 128), bf16),
            pltpu.VMEM((4 * NZ, EXAMPLES * block, 2 * capacity), bf16),
            pltpu.VMEM((chunks, 2 * NZ, block, CHUNK), f32),
            pltpu.VMEM((chunks, 2 * NZ, block, CHUNK), bf16),
            pltpu.VMEM((chunks, 2 * NZ, block, CHUNK), bf16),
            pltpu.VMEM((chunks, NZ, block, CHUNK), bf16),
            pltpu.VMEM((chunks, NZ, block, CHUNK), bf16),
            pltpu.VMEM((chunks, NZ, block, CHUNK), bf16),
            pltpu.VMEM((chunks, NZ, block, CHUNK), bf16),
            pltpu.VMEM((chunks, NZ, block, CHUNK), bf16),
            pltpu.VMEM((chunks, NZ, block, CHUNK), bf16),
            dma((3,)),
            dma((3,)),
            dma((chunks + 1, 31)),
            dma((chunks + 1, 28)),
            dma((chunks, 10)),
            dma((chunks, 10)),
        ],
        compiler_params=pltpu.CompilerParams(
            collective_id=0, has_side_effects=True, vmem_limit_bytes=56 * 2**20
        ),
        cost_estimate=pl.CostEstimate(
            flops=6 * 10**9, bytes_accessed=8 * 2**20, transcendentals=0
        ),
    )(
        expert_ids.reshape(-1, 128),
        probs.reshape(-1, 128),
        example_ids,
        acts.reshape(tokens * slots, hidden),
        grads,
        act_basis[0],
        grad_basis[0],
    )
    return result[None]


def solution(mesh):
    small = mesh.shape["dp"] == 4 * NZ and mesh.shape["expert"] == 2
    return jax.shard_map(
        fused if small else body,
        mesh=mesh,
        in_specs=(
            P(("dp", "expert"), None, None),
            P(("dp", "expert"), None),
            P(("dp", "expert"), None),
            P(("dp", "expert"), None),
            P("dp", "expert"),
            P("expert", "dp", None),
            P("expert", "dp", None),
        ),
        out_specs=P("expert", "dp", None),
        check_vma=False,
    )
```

```python
import math

import jax
import jax.numpy as jnp
from jax import lax
from jax.experimental import pallas as pl
from jax.experimental.pallas import tpu as pltpu
from jax.sharding import PartitionSpec as P

EXAMPLES = 3


def route_block(picked, activity, weights, gradient, labels, expert):
    count_tok = picked.shape[0]
    count_slot = picked.shape[1]
    capacity = count_tok // 4
    names = (picked == expert).astype(jnp.int32)
    named = jnp.sum(names, axis=1, dtype=jnp.int32)
    which = jnp.sum(
        names * jnp.arange(count_slot, dtype=jnp.int32)[None, :], axis=1, dtype=jnp.int32
    )
    ranked = jnp.cumsum(named, dtype=jnp.int32) - 1
    places = jnp.arange(capacity, dtype=jnp.int32)
    table = ((ranked[None, :] == places[:, None]) & (named[None, :] == 1)).astype(jnp.int32)
    token = jnp.sum(
        table * jnp.arange(count_tok, dtype=jnp.int32)[None, :], axis=1, dtype=jnp.int32
    )
    filled = jnp.sum(table, axis=1, dtype=jnp.int32)
    flat_index = token * count_slot + which[token]
    rows_acts = activity.reshape(count_tok * count_slot, activity.shape[-1])[flat_index] * filled[
        :, None
    ].astype(activity.dtype)
    scaled = weights.reshape(count_tok * count_slot)[flat_index] * filled.astype(weights.dtype)
    rows_grads = (scaled[:, None] * gradient[token].astype(jnp.float32)).astype(jnp.bfloat16)
    example_range = jnp.arange(EXAMPLES, dtype=jnp.int32)
    member = ((labels[token][:, None] == example_range[None, :]) & (filled[:, None] == 1)).astype(
        jnp.bfloat16
    )
    return (rows_acts, rows_grads, member)


def body(acts, grads, probs, expert_ids, example_ids, act_basis, grad_basis):
    owners = lax.axis_size("expert")
    shards = lax.axis_size("dp")
    hidden_width = acts.shape[2]
    model_width = grads.shape[1]
    labels = example_ids[0]
    experts = jnp.arange(owners, dtype=jnp.int32)

    def route_one(expert):
        return route_block(expert_ids, acts, probs, grads, labels, expert)

    send_acts, send_grads, send_member = jax.vmap(route_one)(experts)
    got_acts, got_grads, got_member = (
        lax.all_to_all(send_acts, "expert", split_axis=0, concat_axis=0, tiled=True),
        lax.all_to_all(send_grads, "expert", split_axis=0, concat_axis=0, tiled=True),
        lax.all_to_all(send_member, "expert", split_axis=0, concat_axis=0, tiled=True),
    )
    routed_acts = got_acts.reshape(-1, hidden_width)
    routed_grads = got_grads.reshape(-1, model_width)
    member = got_member.reshape(-1, got_member.shape[-1])
    basis_acts = act_basis[0]
    basis_grads = grad_basis[0]
    full_acts, full_grads = (
        lax.all_gather(basis_acts, "dp", axis=0, tiled=True),
        lax.all_gather(basis_grads, "dp", axis=0, tiled=True),
    )
    rotated_acts = jnp.dot(routed_acts, full_acts, preferred_element_type=jnp.float32).astype(
        jnp.bfloat16
    )
    rotated_grads = jnp.dot(routed_grads, full_grads, preferred_element_type=jnp.float32).astype(
        jnp.bfloat16
    )
    scale = 1.0 / (member.shape[-1] * shards)
    member_first = member.T
    width_step = math.gcd(hidden_width, 256)
    pieces = []
    for offset in range(0, hidden_width, width_step):
        columns = lax.dynamic_slice_in_dim(rotated_acts, 0 + offset, width_step, 1)
        masked = member_first[:, :, None] * columns[None, :, :]
        product = jnp.einsum(
            "jrf,rd->jfd", masked, rotated_grads, preferred_element_type=jnp.float32
        )
        pieces.append(jnp.sum(product * product, axis=0))
    totals = jnp.concatenate(pieces, axis=0) * scale
    result = lax.psum_scatter(totals, "dp", scatter_dimension=0, tiled=True)
    return result[None]


NZ = 4
CHUNK = 256


def kernel(
    ids_ref, probs_ref, labels_ref, acts_ref, grads_ref, act_basis_ref, grad_basis_ref, out_ref,
    full_acts, full_grads, send_a, send_g, send_m, rows_a, rows_g, rows_m, masked,
    acc, core_out, core_in, up_out, up_in, down_out, down_in, last_out, last_in,
    y_send, y_recv, x_send, x_recv, g_send, g_recv, r_send, r_recv,
):
    me = lax.axis_index("dp")
    own = lax.axis_index("expert")
    core = lax.rem(me, 2)
    x = lax.rem(me // 2, 2)
    z = me // 4
    chunks = full_grads.shape[0]
    tall = grad_basis_ref.shape[0]
    short = act_basis_ref.shape[0]
    block = out_ref.shape[0]
    capacity = send_a.shape[0]
    bf16, f32 = jnp.bfloat16, jnp.float32

    def at(zz, xx, cc):
        return {"dp": (zz * 2 + xx) * 2 + cc}

    sibling, beside = at(z, x, 1 - core), at(z, 1 - x, core)
    above, below = at(z + 1, x, core), at(z - 1, x, core)
    partner = {"expert": 1 - own}

    barrier = pltpu.get_barrier_semaphore()
    for target in (sibling, beside, partner):
        pl.semaphore_signal(barrier, inc=1, device_id=target, device_id_type=pl.DeviceIdType.MESH)

    @pl.when(z < NZ - 1)
    def _():
        pl.semaphore_signal(barrier, inc=1, device_id=above, device_id_type=pl.DeviceIdType.MESH)

    @pl.when(z > 0)
    def _():
        pl.semaphore_signal(barrier, inc=1, device_id=below, device_id_type=pl.DeviceIdType.MESH)

    ends = (z == 0).astype(jnp.int32) + (z == NZ - 1).astype(jnp.int32)
    pl.semaphore_wait(barrier, 5 - ends)

    def remote(src, dst, ssem, rsem, target):
        return pltpu.make_async_remote_copy(
            src_ref=src, dst_ref=dst, send_sem=ssem, recv_sem=rsem,
            device_id=target, device_id_type=pl.DeviceIdType.MESH,
        )

    half = grad_basis_ref.shape[1] // 2

    def shard(part, zz, xx, cc):
        if part == 0:
            index = (zz * 2 + xx) * 2 + cc
            return full_acts.at[pl.ds(pl.multiple_of(index * short, short), short), :]
        index = cc * NZ + zz
        return full_grads.at[part - 1, pl.ds(pl.multiple_of(index * 2 * tall, tall), 2 * tall), :]

    mine = pl.ds(pl.multiple_of(((core * NZ + z) * 2 + x) * tall, tall), tall)
    theirs = pl.ds(pl.multiple_of(((core * NZ + z) * 2 + 1 - x) * tall, tall), tall)

    def halves(k):
        offset = pl.multiple_of((1 - x) * half + k * CHUNK, CHUNK)
        return remote(
            grad_basis_ref.at[:, pl.ds(offset, CHUNK)], full_grads.at[k, mine, :],
            g_send.at[k + 1, 10], g_recv.at[k + 1, 7], beside,
        )

    def halves_came(k):
        ref = full_grads.at[k, theirs, :]
        remote(ref, ref, g_send.at[k + 1, 10], g_recv.at[k + 1, 7], beside).wait_recv()

    def item_z(item):
        if item == 0:
            return z
        return z - item if item < NZ else z + (item - NZ + 1)

    def present(item):
        if item == 0:
            return z >= 0
        return z >= item if item < NZ else z + (item - NZ + 1) <= NZ - 1

    def copy_up(part, item):
        ref = shard(part, item_z(item), x, core)
        return remote(ref, ref, g_send.at[part, item], g_recv.at[part, item + 1], above)

    def copy_down(part, item):
        new = NZ if item == 0 else item + 1
        ref = shard(part, item_z(item), x, core)
        return remote(ref, ref, g_send.at[part, 3 + new], g_recv.at[part, new], below)

    def copy_beside(part, item):
        ref = shard(part, item_z(item), x, core)
        return remote(ref, ref, g_send.at[part, 10 + item], g_recv.at[part, 7 + item], beside)

    def copy_sibling(part, item):
        ref = shard(part, item_z(item), x, core)
        return remote(ref, ref, g_send.at[part, 17 + item], g_recv.at[part, 14 + item], sibling)

    def copy_sibling_far(part, item):
        ref = shard(part, item_z(item), 1 - x, core)
        return remote(ref, ref, g_send.at[part, 24 + item], g_recv.at[part, 21 + item], sibling)

    def came(part, item, slot, zz, xx, cc):
        ref = shard(part, zz, xx, cc)
        remote(ref, ref, g_send.at[part, 0], g_recv.at[part, slot], sibling).wait_recv()

    def goes_up(item):
        return jnp.logical_and(present(item), z < NZ - 1)

    def goes_down(item):
        return jnp.logical_and(present(item), z > 0)

    def pass_on(part, item):
        @pl.when(present(item))
        def _():
            if item > 0:
                came(part, item, item, item_z(item), x, core)
            elif part > 0:
                halves_came(part - 1)
            if part == 0:
                copy_beside(part, item).start()

        if item < NZ - 1:
            @pl.when(goes_up(item))
            def _():
                copy_up(part, item).start()

        if item == 0 or NZ <= item < 2 * NZ - 2:
            @pl.when(goes_down(item))
            def _():
                copy_down(part, item).start()

        @pl.when(present(item))
        def _():
            copy_sibling(part, item).start()

    def pass_far(part, item):
        @pl.when(present(item))
        def _():
            came(part, item, 7 + item, item_z(item), 1 - x, core)
            copy_sibling_far(part, item).start()

    def hop(part, h):
        for item in ((0,) if h == 0 else (h, NZ - 1 + h)):
            pass_on(part, item)

    def hop_far(part, h):
        for item in ((0,) if h == 0 else (h, NZ - 1 + h)):
            pass_far(part, item)

    def gathered(part):
        for item in range(2 * NZ - 1):
            @pl.when(present(item))
            def _():
                came(part, item, 14 + item, item_z(item), x, 1 - core)
                if part == 0:
                    came(part, item, 21 + item, item_z(item), 1 - x, 1 - core)

    def drain(part):
        for item in range(2 * NZ - 1):
            @pl.when(present(item))
            def _():
                copy_sibling(part, item).wait_send()
                if part == 0:
                    copy_beside(part, item).wait_send()
                    copy_sibling_far(part, item).wait_send()
                elif item == 0:
                    halves(part - 1).wait_send()

            if item < NZ - 1:
                @pl.when(goes_up(item))
                def _():
                    copy_up(part, item).wait_send()

            if item == 0 or NZ <= item < 2 * NZ - 2:
                @pl.when(goes_down(item))
                def _():
                    copy_down(part, item).wait_send()

    def route():
        tokens, slots = ids_ref.shape[1], ids_ref.shape[0]

        def iota(rows, columns, dim):
            return lax.broadcasted_iota(jnp.int32, (rows, columns), dim)

        def ones(mask):
            return jnp.where(mask, 1.0, 0.0).astype(bf16)

        earlier = ones(iota(tokens, tokens, 0) < iota(tokens, tokens, 1))
        spread = ones(iota(tokens, tokens * slots, 0) == iota(tokens, tokens * slots, 1) // slots)
        slot = iota(slots, tokens * slots, 1) % slots == iota(slots, tokens * slots, 0)
        place = iota(capacity, tokens, 0).astype(f32)
        picks, chosen, scales, members = [], [], [], []
        for expert in (1 - own, own):
            hit = jnp.where(ids_ref[...] == expert, 1.0, 0.0)
            named = jnp.sum(hit, axis=0, keepdims=True)
            rank = jnp.dot(
                jnp.broadcast_to(named, hit.shape).astype(bf16), earlier,
                preferred_element_type=f32,
            )
            key = jnp.where(named > 0.5, rank[:1], -1.0)
            table = place == key
            weight = jnp.sum(hit * probs_ref[...], axis=0, keepdims=True)
            scales.append(jnp.sum(jnp.where(table, weight, 0.0), axis=1, keepdims=True))
            label = jnp.sum(jnp.where(table, labels_ref[...] + 1, 0), axis=1, keepdims=True) - 1
            members.append(ones(iota(capacity, 128, 1) == label))
            flat = jnp.dot(hit.astype(bf16), spread, preferred_element_type=f32)
            flat = jnp.sum(jnp.where(slot, flat, 0.0), axis=0, keepdims=True)
            wide = jnp.dot(ones(table), spread, preferred_element_type=f32)
            picks.append((wide * flat).astype(bf16))
            chosen.append(ones(table))
        a = jnp.dot(jnp.concatenate(picks, axis=0), acts_ref[...], preferred_element_type=f32)
        g = jnp.dot(jnp.concatenate(chosen, axis=0), grads_ref[...], preferred_element_type=f32)
        g = (g * jnp.concatenate(scales, axis=0)).astype(bf16)
        g = jnp.concatenate(
            [
                g[:, index * tall : (index + 1) * tall]
                for index in [
                    (zz * 2 + xx) * 2 + cc
                    for cc in range(2) for zz in range(NZ) for xx in range(2)
                ]
            ],
            axis=1,
        )
        send_a[...] = a[:capacity].astype(bf16)
        send_g[...] = g[:capacity]
        send_m[...] = members[0]
        for copy in exchange():
            copy.start()
        rows_a[0] = a[capacity:].astype(bf16)
        rows_g[0] = g[capacity:]
        rows_m[0] = members[1]
        for copy in exchange_x(0):
            copy.start()

    def exchange():
        pairs = ((send_a, rows_a), (send_g, rows_g), (send_m, rows_m))
        return [
            remote(src, dst.at[1], y_send.at[n], y_recv.at[n], partner)
            for n, (src, dst) in enumerate(pairs)
        ]

    def exchange_x(which):
        return [
            remote(
                ref.at[which], ref.at[2 + which],
                x_send.at[which, n], x_recv.at[which, n], beside,
            )
            for n, ref in enumerate((rows_a, rows_g, rows_m))
        ]

    def exchange_on():
        for copy, later in zip(exchange(), exchange_x(1)):
            copy.wait_recv()
            later.start()

    def rotate_acts():
        for which in range(2):
            for copy in exchange_x(which):
                copy.wait_recv()
        rows = rows_a[...].reshape(4 * capacity, rows_a.shape[2])
        rotated = jnp.dot(rows, full_acts[...], preferred_element_type=f32)
        turned = rotated.T.astype(bf16)
        for g in range(2):
            mask = rows_m[2 * g : 2 * g + 2].reshape(2 * capacity, 128)
            mask = mask.astype(f32).T.astype(bf16)
            side = turned[:, g * 2 * capacity : (g + 1) * 2 * capacity]
            for index in range(4 * NZ):
                zz, xx, cc = index // 4, index // 2 % 2, index % 2
                piece = side[index * block : (index + 1) * block, :]
                for j in range(EXAMPLES):
                    start = (j * 2 + xx) * block
                    masked[g, cc * NZ + zz, start : start + block, :] = piece * mask[j : j + 1, :]

    def core_copy(k):
        return remote(core_out.at[k], core_in.at[k], r_send.at[k, 0], r_recv.at[k, 0], sibling)

    def last_copy(k):
        return remote(last_out.at[k], last_in.at[k], r_send.at[k, 1], r_recv.at[k, 1], beside)

    def up_copy(k, b):
        return remote(
            up_out.at[k, b], up_in.at[k, b], r_send.at[k, 2 + b], r_recv.at[k, 2 + b], above
        )

    def down_copy(k, b):
        return remote(
            down_out.at[k, b], down_in.at[k, b], r_send.at[k, 6 + b], r_recv.at[k, 6 + b], below
        )

    def squares(k):
        rows = rows_g[...].reshape(4 * capacity, rows_g.shape[2])
        rotated = jnp.dot(rows, full_grads[k], preferred_element_type=f32).astype(bf16)
        groups = [rotated[g * 2 * capacity : (g + 1) * 2 * capacity] for g in range(2)]

        def total(b):
            result = None
            for g in range(2):
                product = jnp.dot(masked[g, b], groups[g], preferred_element_type=f32)
                for j in range(EXAMPLES):
                    one = product[j * 2 * block : (j + 1) * 2 * block]
                    result = one * one if result is None else result + one * one
            return result

        @pl.loop(0, NZ)
        def _(n):
            core_out[k, n] = total((1 - core) * NZ + n).astype(bf16)

        core_copy(k).start()

        @pl.loop(0, NZ)
        def _(n):
            acc[k, n] = total(core * NZ + n)

    def to_line(k):
        core_copy(k).wait_recv()

        @pl.loop(0, NZ)
        def _(n):
            acc[k, n] = acc[k, n] + core_in[k, n].astype(f32)

        for b in range(NZ):
            @pl.when(jnp.logical_and(z == 0, b > z))
            def _():
                up_out[k, b] = acc[k, b].astype(bf16)
                up_copy(k, b).start()

            @pl.when(jnp.logical_and(z == NZ - 1, b < z))
            def _():
                down_out[k, b] = acc[k, b].astype(bf16)
                down_copy(k, b).start()

    def along(k):
        def up(b):
            @pl.when(jnp.logical_and(z > 0, b > z))
            def _():
                up_copy(k, b).wait_recv()
                up_out[k, b] = (acc[k, b] + up_in[k, b].astype(f32)).astype(bf16)
                up_copy(k, b).start()

        def down(b):
            @pl.when(jnp.logical_and(z < NZ - 1, b < z))
            def _():
                down_copy(k, b).wait_recv()
                down_out[k, b] = (acc[k, b] + down_in[k, b].astype(f32)).astype(bf16)
                down_copy(k, b).start()

        for b in range(NZ):
            up(NZ - 1 - b)
            down(b)

    def finish(k):
        for b in range(NZ):
            @pl.when(jnp.logical_and(z > 0, z == b))
            def _():
                up_copy(k, b).wait_recv()
                acc[k, b] = acc[k, b] + up_in[k, b].astype(f32)

            @pl.when(jnp.logical_and(z < NZ - 1, z == b))
            def _():
                down_copy(k, b).wait_recv()
                acc[k, b] = acc[k, b] + down_in[k, b].astype(f32)

        scale = 1.0 / (EXAMPLES * 4 * NZ)
        near = pl.ds(pl.multiple_of(x * block, block), block)
        far = pl.ds(pl.multiple_of((1 - x) * block, block), block)
        last_out[k] = acc[k, z, far, :] * scale
        last_copy(k).start()
        columns = pl.ds(pl.multiple_of(x * half + k * CHUNK, CHUNK), CHUNK)
        out_ref[:, columns] = acc[k, z, near, :] * scale

    def place_last(k):
        last_copy(k).wait_recv()
        columns = pl.ds(pl.multiple_of((1 - x) * half + k * CHUNK, CHUNK), CHUNK)
        out_ref[:, columns] = last_in[k]

    def drain_sums(k):
        core_copy(k).wait_send()
        last_copy(k).wait_send()
        for b in range(NZ):
            @pl.when(jnp.logical_and(z < NZ - 1, b > z))
            def _():
                up_copy(k, b).wait_send()

            @pl.when(jnp.logical_and(z > 0, b < z))
            def _():
                down_copy(k, b).wait_send()

    parts = chunks + 1
    ahead = 2
    full_acts[pl.ds(pl.multiple_of(me * short, short), short), :] = act_basis_ref[...]
    hop(0, 0)
    for k in range(chunks):
        halves(k).start()
    for k in range(chunks):
        offset = pl.multiple_of(x * half + k * CHUNK, CHUNK)
        full_grads[k, mine, :] = grad_basis_ref[:, pl.ds(offset, CHUNK)]
    hop(1, 0)
    for step in range(parts + NZ + 4):
        if step + ahead < parts:
            hop(step + ahead, 0)
        if step == 0:
            route()
        for h in range(1, NZ):
            if 0 <= step - h < parts:
                hop(step - h, h)
        if step == 1:
            exchange_on()
        for h in range(NZ):
            if step - h - 1 == 0:
                hop_far(0, h)
        if 0 <= step - NZ < parts:
            gathered(step - NZ)
            if step == NZ:
                rotate_acts()
            else:
                squares(step - NZ - 1)
        if 0 <= step - NZ - 2 < chunks:
            to_line(step - NZ - 2)
        if 0 <= step - NZ - 3 < chunks:
            along(step - NZ - 3)
        if 0 <= step - NZ - 3 < chunks:
            finish(step - NZ - 3)
        if 0 <= step - NZ - 4 < chunks:
            place_last(step - NZ - 4)
    for which in range(2):
        for copy in exchange_x(which):
            copy.wait_send()
    for copy in exchange():
        copy.wait_send()
    for part in range(parts):
        drain(part)
    for k in range(chunks):
        drain_sums(k)


def fused(acts, grads, probs, expert_ids, example_ids, act_basis, grad_basis):
    tokens, slots, hidden = acts.shape
    model = grads.shape[1]
    capacity = tokens // 4
    chunks = model // 2 // CHUNK
    block = hidden // (4 * NZ)
    bf16, f32 = jnp.bfloat16, jnp.float32
    vm = pl.BlockSpec(memory_space=pltpu.VMEM)
    dma = pltpu.SemaphoreType.DMA
    result = pl.pallas_call(
        kernel,
        out_shape=jax.ShapeDtypeStruct((block, model), f32),
        in_specs=[vm] * 7,
        out_specs=vm,
        scratch_shapes=[
            pltpu.VMEM((hidden, hidden), bf16),
            pltpu.VMEM((chunks, model, CHUNK), bf16),
            pltpu.VMEM((capacity, hidden), bf16),
            pltpu.VMEM((capacity, model), bf16),
            pltpu.VMEM((capacity, 128), bf16),
            pltpu.VMEM((4, capacity, hidden), bf16),
            pltpu.VMEM((4, capacity, model), bf16),
            pltpu.VMEM((4, capacity, 128), bf16),
            pltpu.VMEM((2, 2 * NZ, EXAMPLES * 2 * block, 2 * capacity), bf16),
            pltpu.VMEM((chunks, NZ, 2 * block, CHUNK), f32),
            pltpu.VMEM((chunks, NZ, 2 * block, CHUNK), bf16),
            pltpu.VMEM((chunks, NZ, 2 * block, CHUNK), bf16),
            pltpu.VMEM((chunks, NZ, 2 * block, CHUNK), bf16),
            pltpu.VMEM((chunks, NZ, 2 * block, CHUNK), bf16),
            pltpu.VMEM((chunks, NZ, 2 * block, CHUNK), bf16),
            pltpu.VMEM((chunks, NZ, 2 * block, CHUNK), bf16),
            pltpu.VMEM((chunks, block, CHUNK), f32),
            pltpu.VMEM((chunks, block, CHUNK), f32),
            dma((3,)),
            dma((3,)),
            dma((2, 3)),
            dma((2, 3)),
            dma((chunks + 1, 31)),
            dma((chunks + 1, 28)),
            dma((chunks, 10)),
            dma((chunks, 10)),
        ],
        compiler_params=pltpu.CompilerParams(
            collective_id=0, has_side_effects=True, vmem_limit_bytes=56 * 2**20
        ),
        cost_estimate=pl.CostEstimate(
            flops=6 * 10**9, bytes_accessed=8 * 2**20, transcendentals=0
        ),
    )(
        expert_ids.T,
        probs.T,
        example_ids,
        acts.reshape(tokens * slots, hidden),
        grads,
        act_basis[0],
        grad_basis[0],
    )
    return result[None]


def solution(mesh):
    small = mesh.shape["dp"] == 4 * NZ and mesh.shape["expert"] == 2
    return jax.shard_map(
        fused if small else body,
        mesh=mesh,
        in_specs=(
            P(("dp", "expert"), None, None),
            P(("dp", "expert"), None),
            P(("dp", "expert"), None),
            P(("dp", "expert"), None),
            P("dp", "expert"),
            P("expert", "dp", None),
            P("expert", "dp", None),
        ),
        out_specs=P("expert", "dp", None),
        check_vma=False,
    )
```

```python
import math

import jax
import jax.numpy as jnp
from jax import lax
from jax.experimental import pallas as pl
from jax.experimental.pallas import tpu as pltpu
from jax.sharding import PartitionSpec as P

EXAMPLES = 3


def route_block(picked, activity, weights, gradient, labels, expert):
    count_tok = picked.shape[0]
    count_slot = picked.shape[1]
    capacity = count_tok // 4
    names = (picked == expert).astype(jnp.int32)
    named = jnp.sum(names, axis=1, dtype=jnp.int32)
    which = jnp.sum(
        names * jnp.arange(count_slot, dtype=jnp.int32)[None, :], axis=1, dtype=jnp.int32
    )
    ranked = jnp.cumsum(named, dtype=jnp.int32) - 1
    places = jnp.arange(capacity, dtype=jnp.int32)
    table = ((ranked[None, :] == places[:, None]) & (named[None, :] == 1)).astype(jnp.int32)
    token = jnp.sum(
        table * jnp.arange(count_tok, dtype=jnp.int32)[None, :], axis=1, dtype=jnp.int32
    )
    filled = jnp.sum(table, axis=1, dtype=jnp.int32)
    flat_index = token * count_slot + which[token]
    rows_acts = activity.reshape(count_tok * count_slot, activity.shape[-1])[flat_index] * filled[
        :, None
    ].astype(activity.dtype)
    scaled = weights.reshape(count_tok * count_slot)[flat_index] * filled.astype(weights.dtype)
    rows_grads = (scaled[:, None] * gradient[token].astype(jnp.float32)).astype(jnp.bfloat16)
    example_range = jnp.arange(EXAMPLES, dtype=jnp.int32)
    member = ((labels[token][:, None] == example_range[None, :]) & (filled[:, None] == 1)).astype(
        jnp.bfloat16
    )
    return (rows_acts, rows_grads, member)


def body(acts, grads, probs, expert_ids, example_ids, act_basis, grad_basis):
    owners = lax.axis_size("expert")
    shards = lax.axis_size("dp")
    hidden_width = acts.shape[2]
    model_width = grads.shape[1]
    labels = example_ids[0]
    experts = jnp.arange(owners, dtype=jnp.int32)

    def route_one(expert):
        return route_block(expert_ids, acts, probs, grads, labels, expert)

    send_acts, send_grads, send_member = jax.vmap(route_one)(experts)
    got_acts, got_grads, got_member = (
        lax.all_to_all(send_acts, "expert", split_axis=0, concat_axis=0, tiled=True),
        lax.all_to_all(send_grads, "expert", split_axis=0, concat_axis=0, tiled=True),
        lax.all_to_all(send_member, "expert", split_axis=0, concat_axis=0, tiled=True),
    )
    routed_acts = got_acts.reshape(-1, hidden_width)
    routed_grads = got_grads.reshape(-1, model_width)
    member = got_member.reshape(-1, got_member.shape[-1])
    basis_acts = act_basis[0]
    basis_grads = grad_basis[0]
    full_acts, full_grads = (
        lax.all_gather(basis_acts, "dp", axis=0, tiled=True),
        lax.all_gather(basis_grads, "dp", axis=0, tiled=True),
    )
    rotated_acts = jnp.dot(routed_acts, full_acts, preferred_element_type=jnp.float32).astype(
        jnp.bfloat16
    )
    rotated_grads = jnp.dot(routed_grads, full_grads, preferred_element_type=jnp.float32).astype(
        jnp.bfloat16
    )
    scale = 1.0 / (member.shape[-1] * shards)
    member_first = member.T
    width_step = math.gcd(hidden_width, 256)
    pieces = []
    for offset in range(0, hidden_width, width_step):
        columns = lax.dynamic_slice_in_dim(rotated_acts, 0 + offset, width_step, 1)
        masked = member_first[:, :, None] * columns[None, :, :]
        product = jnp.einsum(
            "jrf,rd->jfd", masked, rotated_grads, preferred_element_type=jnp.float32
        )
        pieces.append(jnp.sum(product * product, axis=0))
    totals = jnp.concatenate(pieces, axis=0) * scale
    result = lax.psum_scatter(totals, "dp", scatter_dimension=0, tiled=True)
    return result[None]


NZ = 4
CHUNK = 256


def kernel(
    ids_ref, probs_ref, labels_ref, acts_ref, grads_ref, act_basis_ref, grad_basis_ref, out_ref,
    full_acts, full_grads, send_a, send_g, send_m, rows_a, rows_g, rows_m, masked,
    acc, core_out, core_in, up_out, up_in, down_out, down_in, last_out, last_in,
    y_send, y_recv, x_send, x_recv, g_send, g_recv, r_send, r_recv,
):
    me = lax.axis_index("dp")
    own = lax.axis_index("expert")
    core = lax.rem(me, 2)
    x = lax.rem(me // 2, 2)
    z = me // 4
    chunks = full_grads.shape[0]
    tall = grad_basis_ref.shape[0]
    short = act_basis_ref.shape[0]
    block = out_ref.shape[0]
    capacity = send_a.shape[0]
    bf16, f32 = jnp.bfloat16, jnp.float32

    def at(zz, xx, cc):
        return {"dp": (zz * 2 + xx) * 2 + cc}

    sibling, beside = at(z, x, 1 - core), at(z, 1 - x, core)
    above, below = at(z + 1, x, core), at(z - 1, x, core)
    partner = {"expert": 1 - own}

    barrier = pltpu.get_barrier_semaphore()
    for target in (beside, partner):
        pl.semaphore_signal(barrier, inc=1, device_id=target, device_id_type=pl.DeviceIdType.MESH)

    @pl.when(z < NZ - 1)
    def _():
        pl.semaphore_signal(barrier, inc=1, device_id=above, device_id_type=pl.DeviceIdType.MESH)

    @pl.when(z > 0)
    def _():
        pl.semaphore_signal(barrier, inc=1, device_id=below, device_id_type=pl.DeviceIdType.MESH)

    ends = (z == 0).astype(jnp.int32) + (z == NZ - 1).astype(jnp.int32)
    pl.semaphore_wait(barrier, 4 - ends + core)
    pl.semaphore_signal(barrier, inc=1, device_id=sibling, device_id_type=pl.DeviceIdType.MESH)

    def meet_sibling():
        @pl.when(core == 0)
        def _():
            pl.semaphore_wait(barrier, 1)

    def remote(src, dst, ssem, rsem, target):
        return pltpu.make_async_remote_copy(
            src_ref=src, dst_ref=dst, send_sem=ssem, recv_sem=rsem,
            device_id=target, device_id_type=pl.DeviceIdType.MESH,
        )

    half = grad_basis_ref.shape[1] // 2

    def shard(part, zz, xx, cc):
        if part == 0:
            index = (zz * 2 + xx) * 2 + cc
            return full_acts.at[pl.ds(pl.multiple_of(index * short, short), short), :]
        index = cc * NZ + zz
        return full_grads.at[part - 1, pl.ds(pl.multiple_of(index * 2 * tall, tall), 2 * tall), :]

    mine = pl.ds(pl.multiple_of(((core * NZ + z) * 2 + x) * tall, tall), tall)
    theirs = pl.ds(pl.multiple_of(((core * NZ + z) * 2 + 1 - x) * tall, tall), tall)

    def halves(k):
        offset = pl.multiple_of((1 - x) * half + k * CHUNK, CHUNK)
        return remote(
            grad_basis_ref.at[:, pl.ds(offset, CHUNK)], full_grads.at[k, mine, :],
            g_send.at[k + 1, 10], g_recv.at[k + 1, 7], beside,
        )

    def halves_came(k):
        ref = full_grads.at[k, theirs, :]
        remote(ref, ref, g_send.at[k + 1, 10], g_recv.at[k + 1, 7], beside).wait_recv()

    def item_z(item):
        if item == 0:
            return z
        return z - item if item < NZ else z + (item - NZ + 1)

    def present(item):
        if item == 0:
            return z >= 0
        return z >= item if item < NZ else z + (item - NZ + 1) <= NZ - 1

    def copy_up(part, item):
        ref = shard(part, item_z(item), x, core)
        return remote(ref, ref, g_send.at[part, item], g_recv.at[part, item + 1], above)

    def copy_down(part, item):
        new = NZ if item == 0 else item + 1
        ref = shard(part, item_z(item), x, core)
        return remote(ref, ref, g_send.at[part, 3 + new], g_recv.at[part, new], below)

    def copy_beside(part, item):
        ref = shard(part, item_z(item), x, core)
        return remote(ref, ref, g_send.at[part, 10 + item], g_recv.at[part, 7 + item], beside)

    def copy_sibling(part, item):
        ref = shard(part, item_z(item), x, core)
        return remote(ref, ref, g_send.at[part, 17 + item], g_recv.at[part, 14 + item], sibling)

    def copy_sibling_far(part, item):
        ref = shard(part, item_z(item), 1 - x, core)
        return remote(ref, ref, g_send.at[part, 24 + item], g_recv.at[part, 21 + item], sibling)

    def came(part, item, slot, zz, xx, cc):
        ref = shard(part, zz, xx, cc)
        remote(ref, ref, g_send.at[part, 0], g_recv.at[part, slot], sibling).wait_recv()

    def goes_up(item):
        return jnp.logical_and(present(item), z < NZ - 1)

    def goes_down(item):
        return jnp.logical_and(present(item), z > 0)

    def pass_on(part, item):
        @pl.when(present(item))
        def _():
            if item > 0:
                came(part, item, item, item_z(item), x, core)
            elif part > 0:
                halves_came(part - 1)
            if part == 0:
                copy_beside(part, item).start()

        if item < NZ - 1:
            @pl.when(goes_up(item))
            def _():
                copy_up(part, item).start()

        if item == 0 or NZ <= item < 2 * NZ - 2:
            @pl.when(goes_down(item))
            def _():
                copy_down(part, item).start()

    def share(part, h):
        for item in ((0,) if h == 0 else (h, NZ - 1 + h)):
            @pl.when(present(item))
            def _():
                copy_sibling(part, item).start()

    def pass_far(part, item):
        @pl.when(present(item))
        def _():
            came(part, item, 7 + item, item_z(item), 1 - x, core)
            copy_sibling_far(part, item).start()

    def hop(part, h):
        for item in ((0,) if h == 0 else (h, NZ - 1 + h)):
            pass_on(part, item)

    def hop_far(part, h):
        for item in ((0,) if h == 0 else (h, NZ - 1 + h)):
            pass_far(part, item)

    def gathered(part):
        for item in range(2 * NZ - 1):
            @pl.when(present(item))
            def _():
                came(part, item, 14 + item, item_z(item), x, 1 - core)
                if part == 0:
                    came(part, item, 21 + item, item_z(item), 1 - x, 1 - core)

    def drain(part):
        for item in range(2 * NZ - 1):
            @pl.when(present(item))
            def _():
                copy_sibling(part, item).wait_send()
                if part == 0:
                    copy_beside(part, item).wait_send()
                    copy_sibling_far(part, item).wait_send()
                elif item == 0:
                    halves(part - 1).wait_send()

            if item < NZ - 1:
                @pl.when(goes_up(item))
                def _():
                    copy_up(part, item).wait_send()

            if item == 0 or NZ <= item < 2 * NZ - 2:
                @pl.when(goes_down(item))
                def _():
                    copy_down(part, item).wait_send()

    def route():
        tokens, slots = ids_ref.shape[1], ids_ref.shape[0]

        def iota(rows, columns, dim):
            return lax.broadcasted_iota(jnp.int32, (rows, columns), dim)

        def ones(mask):
            return jnp.where(mask, 1.0, 0.0).astype(bf16)

        earlier = ones(iota(tokens, tokens, 0) < iota(tokens, tokens, 1))
        spread = ones(iota(tokens, tokens * slots, 0) == iota(tokens, tokens * slots, 1) // slots)
        slot = iota(slots, tokens * slots, 1) % slots == iota(slots, tokens * slots, 0)
        place = iota(capacity, tokens, 0).astype(f32)
        picks, chosen, scales, members = [], [], [], []
        for expert in (1 - own, own):
            hit = jnp.where(ids_ref[...] == expert, 1.0, 0.0)
            named = jnp.sum(hit, axis=0, keepdims=True)
            rank = jnp.dot(
                jnp.broadcast_to(named, hit.shape).astype(bf16), earlier,
                preferred_element_type=f32,
            )
            key = jnp.where(named > 0.5, rank[:1], -1.0)
            table = place == key
            weight = jnp.sum(hit * probs_ref[...], axis=0, keepdims=True)
            scales.append(jnp.sum(jnp.where(table, weight, 0.0), axis=1, keepdims=True))
            label = jnp.sum(jnp.where(table, labels_ref[...] + 1, 0), axis=1, keepdims=True) - 1
            members.append(ones(iota(capacity, 128, 1) == label))
            flat = jnp.dot(hit.astype(bf16), spread, preferred_element_type=f32)
            flat = jnp.sum(jnp.where(slot, flat, 0.0), axis=0, keepdims=True)
            wide = jnp.dot(ones(table), spread, preferred_element_type=f32)
            picks.append((wide * flat).astype(bf16))
            chosen.append(ones(table))
        a = jnp.dot(jnp.concatenate(picks, axis=0), acts_ref[...], preferred_element_type=f32)
        g = jnp.dot(jnp.concatenate(chosen, axis=0), grads_ref[...], preferred_element_type=f32)
        g = (g * jnp.concatenate(scales, axis=0)).astype(bf16)
        g = jnp.concatenate(
            [
                g[:, index * tall : (index + 1) * tall]
                for index in [
                    (zz * 2 + xx) * 2 + cc
                    for cc in range(2) for zz in range(NZ) for xx in range(2)
                ]
            ],
            axis=1,
        )
        send_a[...] = a[:capacity].astype(bf16)
        send_g[...] = g[:capacity]
        send_m[...] = members[0]
        for copy in exchange():
            copy.start()
        rows_a[0] = a[capacity:].astype(bf16)
        rows_g[0] = g[capacity:]
        rows_m[0] = members[1]
        for copy in exchange_x(0):
            copy.start()

    def exchange():
        pairs = ((send_a, rows_a), (send_g, rows_g), (send_m, rows_m))
        return [
            remote(src, dst.at[1], y_send.at[n], y_recv.at[n], partner)
            for n, (src, dst) in enumerate(pairs)
        ]

    def exchange_x(which):
        return [
            remote(
                ref.at[which], ref.at[2 + which],
                x_send.at[which, n], x_recv.at[which, n], beside,
            )
            for n, ref in enumerate((rows_a, rows_g, rows_m))
        ]

    def exchange_on():
        for copy, later in zip(exchange(), exchange_x(1)):
            copy.wait_recv()
            later.start()

    def rotate_acts():
        for which in range(2):
            for copy in exchange_x(which):
                copy.wait_recv()
        rows = rows_a[...].reshape(4 * capacity, rows_a.shape[2])
        rotated = jnp.dot(rows, full_acts[...], preferred_element_type=f32)
        turned = rotated.T.astype(bf16)
        for g in range(2):
            mask = rows_m[2 * g : 2 * g + 2].reshape(2 * capacity, 128)
            mask = mask.astype(f32).T.astype(bf16)
            side = turned[:, g * 2 * capacity : (g + 1) * 2 * capacity]
            for index in range(4 * NZ):
                zz, xx, cc = index // 4, index // 2 % 2, index % 2
                piece = side[index * block : (index + 1) * block, :]
                for j in range(EXAMPLES):
                    start = (j * 2 + xx) * block
                    masked[g, cc * NZ + zz, start : start + block, :] = piece * mask[j : j + 1, :]

    def core_copy(k):
        return remote(core_out.at[k], core_in.at[k], r_send.at[k, 0], r_recv.at[k, 0], sibling)

    def last_copy(k):
        return remote(last_out.at[k], last_in.at[k], r_send.at[k, 1], r_recv.at[k, 1], beside)

    def up_copy(k, b):
        return remote(
            up_out.at[k, b], up_in.at[k, b], r_send.at[k, 2 + b], r_recv.at[k, 2 + b], above
        )

    def down_copy(k, b):
        return remote(
            down_out.at[k, b], down_in.at[k, b], r_send.at[k, 6 + b], r_recv.at[k, 6 + b], below
        )

    def squares(k):
        rows = rows_g[...].reshape(4 * capacity, rows_g.shape[2])
        rotated = jnp.dot(rows, full_grads[k], preferred_element_type=f32).astype(bf16)
        groups = [rotated[g * 2 * capacity : (g + 1) * 2 * capacity] for g in range(2)]

        def total(b):
            result = None
            for g in range(2):
                product = jnp.dot(masked[g, b], groups[g], preferred_element_type=f32)
                for j in range(EXAMPLES):
                    one = product[j * 2 * block : (j + 1) * 2 * block]
                    result = one * one if result is None else result + one * one
            return result

        @pl.loop(0, NZ)
        def _(n):
            core_out[k, n] = total((1 - core) * NZ + n).astype(bf16)

        core_copy(k).start()

        @pl.loop(0, NZ)
        def _(n):
            acc[k, n] = total(core * NZ + n)

    def to_line(k):
        core_copy(k).wait_recv()

        @pl.loop(0, NZ)
        def _(n):
            acc[k, n] = acc[k, n] + core_in[k, n].astype(f32)

        for b in range(NZ):
            @pl.when(jnp.logical_and(z == 0, b > z))
            def _():
                up_out[k, b] = acc[k, b].astype(bf16)
                up_copy(k, b).start()

            @pl.when(jnp.logical_and(z == NZ - 1, b < z))
            def _():
                down_out[k, b] = acc[k, b].astype(bf16)
                down_copy(k, b).start()

    def along(k):
        def up(b):
            @pl.when(jnp.logical_and(z > 0, b > z))
            def _():
                up_copy(k, b).wait_recv()
                up_out[k, b] = (acc[k, b] + up_in[k, b].astype(f32)).astype(bf16)
                up_copy(k, b).start()

        def down(b):
            @pl.when(jnp.logical_and(z < NZ - 1, b < z))
            def _():
                down_copy(k, b).wait_recv()
                down_out[k, b] = (acc[k, b] + down_in[k, b].astype(f32)).astype(bf16)
                down_copy(k, b).start()

        for b in range(NZ):
            up(NZ - 1 - b)
            down(b)

    def finish(k):
        for b in range(NZ):
            @pl.when(jnp.logical_and(z > 0, z == b))
            def _():
                up_copy(k, b).wait_recv()
                acc[k, b] = acc[k, b] + up_in[k, b].astype(f32)

            @pl.when(jnp.logical_and(z < NZ - 1, z == b))
            def _():
                down_copy(k, b).wait_recv()
                acc[k, b] = acc[k, b] + down_in[k, b].astype(f32)

        scale = 1.0 / (EXAMPLES * 4 * NZ)
        near = pl.ds(pl.multiple_of(x * block, block), block)
        far = pl.ds(pl.multiple_of((1 - x) * block, block), block)
        last_out[k] = acc[k, z, far, :] * scale
        last_copy(k).start()
        columns = pl.ds(pl.multiple_of(x * half + k * CHUNK, CHUNK), CHUNK)
        out_ref[:, columns] = acc[k, z, near, :] * scale

    def place_last(k):
        last_copy(k).wait_recv()
        columns = pl.ds(pl.multiple_of((1 - x) * half + k * CHUNK, CHUNK), CHUNK)
        out_ref[:, columns] = last_in[k]

    def drain_sums(k):
        core_copy(k).wait_send()
        last_copy(k).wait_send()
        for b in range(NZ):
            @pl.when(jnp.logical_and(z < NZ - 1, b > z))
            def _():
                up_copy(k, b).wait_send()

            @pl.when(jnp.logical_and(z > 0, b < z))
            def _():
                down_copy(k, b).wait_send()

    parts = chunks + 1
    ahead = 2
    full_acts[pl.ds(pl.multiple_of(me * short, short), short), :] = act_basis_ref[...]
    hop(0, 0)
    for k in range(chunks):
        halves(k).start()
    for k in range(chunks):
        offset = pl.multiple_of(x * half + k * CHUNK, CHUNK)
        full_grads[k, mine, :] = grad_basis_ref[:, pl.ds(offset, CHUNK)]
    hop(1, 0)
    met = 2
    waiting = [(0, 0), (1, 0)]
    for step in range(parts + NZ + 4):
        if step + ahead < parts:
            hop(step + ahead, 0)
            waiting.append((step + ahead, 0))
        if step == 0:
            route()
        for h in range(1, NZ):
            if 0 <= step - h < parts:
                hop(step - h, h)
                waiting.append((step - h, h))
        if step == 1:
            exchange_on()
        if step == met:
            meet_sibling()
        if step >= met:
            for part, h in waiting:
                share(part, h)
            waiting = []
            for h in range(NZ):
                if step - h - 1 == 0 or (step == met and h < step - 1):
                    hop_far(0, h)
        if 0 <= step - NZ < parts:
            gathered(step - NZ)
            if step == NZ:
                rotate_acts()
            else:
                squares(step - NZ - 1)
        if 0 <= step - NZ - 2 < chunks:
            to_line(step - NZ - 2)
        if 0 <= step - NZ - 3 < chunks:
            along(step - NZ - 3)
        if 0 <= step - NZ - 3 < chunks:
            finish(step - NZ - 3)
        if 0 <= step - NZ - 4 < chunks:
            place_last(step - NZ - 4)
    for which in range(2):
        for copy in exchange_x(which):
            copy.wait_send()
    for copy in exchange():
        copy.wait_send()
    for part in range(parts):
        drain(part)
    for k in range(chunks):
        drain_sums(k)


def fused(acts, grads, probs, expert_ids, example_ids, act_basis, grad_basis):
    tokens, slots, hidden = acts.shape
    model = grads.shape[1]
    capacity = tokens // 4
    chunks = model // 2 // CHUNK
    block = hidden // (4 * NZ)
    bf16, f32 = jnp.bfloat16, jnp.float32
    vm = pl.BlockSpec(memory_space=pltpu.VMEM)
    dma = pltpu.SemaphoreType.DMA
    result = pl.pallas_call(
        kernel,
        out_shape=jax.ShapeDtypeStruct((block, model), f32),
        in_specs=[vm] * 7,
        out_specs=vm,
        scratch_shapes=[
            pltpu.VMEM((hidden, hidden), bf16),
            pltpu.VMEM((chunks, model, CHUNK), bf16),
            pltpu.VMEM((capacity, hidden), bf16),
            pltpu.VMEM((capacity, model), bf16),
            pltpu.VMEM((capacity, 128), bf16),
            pltpu.VMEM((4, capacity, hidden), bf16),
            pltpu.VMEM((4, capacity, model), bf16),
            pltpu.VMEM((4, capacity, 128), bf16),
            pltpu.VMEM((2, 2 * NZ, EXAMPLES * 2 * block, 2 * capacity), bf16),
            pltpu.VMEM((chunks, NZ, 2 * block, CHUNK), f32),
            pltpu.VMEM((chunks, NZ, 2 * block, CHUNK), bf16),
            pltpu.VMEM((chunks, NZ, 2 * block, CHUNK), bf16),
            pltpu.VMEM((chunks, NZ, 2 * block, CHUNK), bf16),
            pltpu.VMEM((chunks, NZ, 2 * block, CHUNK), bf16),
            pltpu.VMEM((chunks, NZ, 2 * block, CHUNK), bf16),
            pltpu.VMEM((chunks, NZ, 2 * block, CHUNK), bf16),
            pltpu.VMEM((chunks, block, CHUNK), f32),
            pltpu.VMEM((chunks, block, CHUNK), f32),
            dma((3,)),
            dma((3,)),
            dma((2, 3)),
            dma((2, 3)),
            dma((chunks + 1, 31)),
            dma((chunks + 1, 28)),
            dma((chunks, 10)),
            dma((chunks, 10)),
        ],
        compiler_params=pltpu.CompilerParams(
            collective_id=0, has_side_effects=True, vmem_limit_bytes=56 * 2**20
        ),
        cost_estimate=pl.CostEstimate(
            flops=6 * 10**9, bytes_accessed=8 * 2**20, transcendentals=0
        ),
    )(
        expert_ids.T,
        probs.T,
        example_ids,
        acts.reshape(tokens * slots, hidden),
        grads,
        act_basis[0],
        grad_basis[0],
    )
    return result[None]


def solution(mesh):
    small = mesh.shape["dp"] == 4 * NZ and mesh.shape["expert"] == 2
    return jax.shard_map(
        fused if small else body,
        mesh=mesh,
        in_specs=(
            P(("dp", "expert"), None, None),
            P(("dp", "expert"), None),
            P(("dp", "expert"), None),
            P(("dp", "expert"), None),
            P("dp", "expert"),
            P("expert", "dp", None),
            P("expert", "dp", None),
        ),
        out_specs=P("expert", "dp", None),
        check_vma=False,
    )
```
